32 devices in a mesh: groups: 2 (over y), mp: 8 (over z, x), batch: 2 (over core).
Axes of the slice: x: 2, y: 2, z: 4, core: 2. Of those that a mesh axis runs over, the one named last changes fastest.
Arguments:
- byte_ids: int32 [3, 1024], P(None, ('groups', 'batch')), parts along dimension 1, may hold values from 0 to 255
- h_start: bfloat16 [1024, 4096], P(('groups', 'batch'), 'mp'), parts along dimension 0, may hold values from -0.8984375 to 0.8984375
- c_start: float32 [1024, 4096], P(('groups', 'batch'), 'mp'), parts along dimension 0, may hold values from -4 to 4
- inter_weight: bfloat16 [4096, 4096], P('mp'), may hold values from -0.375 to 0.375
- inter_embed: bfloat16 [256, 4096], P(None, 'mp'), may hold values from -4 to 4
- gate_weight: bfloat16 [4096, 16384], P(None, 'mp'), may hold values from -0.1875 to 0.1875
- gate_embed: bfloat16 [256, 16384], P(None, 'mp'), may hold values from -3 to 3
- gate_bias: float32 [16384], P('mp'), may hold values from -3 to 3
Outputs:
- h_final: bfloat16 [1024, 4096], P(('groups', 'batch'), 'mp'), parts along dimension 0
- c_final: float32 [1024, 4096], P(('groups', 'batch'), 'mp'), parts along dimension 0
The draws below stay inside these ranges and needn't reach their ends.
There are 2 independent parts, one for each index of `groups`. The reference program is written for one: setup_inputs(seed, part) draws one part's arguments, and reference() takes and returns one part's arrays. A program takes and returns all parts, laid end to end along the dimension named above; an argument that names none is the same for every part. Nothing has to cross between parts.
All inputs are finite; a program needn't handle non-finite values.
Results may differ from the reference program's by a relative error of at most 0.015.
Values may be sent and summed in bfloat16 or wider, within the bound.
No kernel may reach another device: no remote copies, remote signals or barrier semaphores. Data moves between devices by JAX's collectives and lax.ppermute only.
A program may use at most 128 MiB of HBM per device.

```python
import math
import jax
import jax.numpy as jnp
import numpy as np
from jax import lax

H = 4096
M = 4096
VOCAB = 256
STEPS = 3
STREAMS = 512
GATES = 16384


def place_ends(array, rng, low, top_value):
    index_at = [jax.random.randint(jax.random.fold_in(rng, axis), (), 0, length) for axis, length in enumerate(array.shape)]
    longest = array.shape.index(max(array.shape))
    beside = index_at[:longest] + [(index_at[longest] + 1) % array.shape[longest]] + index_at[longest + 1:]
    return array.at[tuple(index_at)].set(low).at[tuple(beside)].set(top_value)


def block_scale(key, dims, split, low, high):
    def one(axis_at, blocks):
        draws = jax.random.uniform(jax.random.fold_in(jax.random.fold_in(key, 6), axis_at), (blocks,), jnp.float32, low / len(split), high / len(split))
        return jnp.repeat(jnp.exp(draws), dims[axis_at] // blocks).reshape((-1,) + (1,) * (len(dims) - axis_at - 1))

    loudness = one(*split[0])
    for cut in split[1:]:
        loudness = loudness * one(*cut)
    return loudness


def rank_bounds(number_of, lean):
    weights = [(1 << 20) // math.isqrt(grade ** lean) + 1 for grade in range(1, number_of + 1)]
    width = 1 + sum(weights) // (1 << 30)
    return np.cumsum(np.array([max(1, weight // width) for weight in weights]))


def ranked_ids(rng, shape, count, lean):
    table = rank_bounds(count, lean)
    lot = jax.random.randint(jax.random.fold_in(rng, 1), shape, 0, int(table[count - 1]))
    standing = jnp.searchsorted(jnp.asarray(table, jnp.int32), lot, side="right")
    return jax.random.permutation(jax.random.fold_in(rng, 2), count)[standing].astype(jnp.int32)


def gaussian(rng, dims, width, limit, split=(), held_as=jnp.bfloat16):
    entries = jax.random.normal(rng, dims, jnp.float32) * width
    if len(split) > 0:
        entries = block_scale(rng, dims, split, -0.22, 0.18) * entries
    return jnp.clip(entries, min=-limit, max=limit).astype(held_as)


def setup_inputs(seed: int = 0, part: int = 0) -> dict:
    key_of = jax.random.split(jax.random.key(seed), 9)
    part_splits = jax.random.split(jax.random.fold_in(key_of[8], part), 9)
    return {
        "byte_ids": place_ends(ranked_ids(part_splits[0], (STEPS, STREAMS), VOCAB, 2), jax.random.fold_in(part_splits[0], 3), 0, VOCAB - 1).astype(jnp.int32),
        "h_start": jnp.clip(jax.random.uniform(part_splits[1], (STREAMS, H), jnp.float32, -0.8984375, 0.8984375) * block_scale(part_splits[1], (STREAMS, H), ((0, 2), (1, 8)), -0.4, 0.0), -0.8984375, 0.8984375).astype(jnp.bfloat16),
        "c_start": gaussian(part_splits[2], (STREAMS, H), 1.0, 4.0, ((0, 2), (1, 8)), jnp.float32),
        "inter_weight": gaussian(key_of[3], (M, H), (H // 16) ** -0.5, 0.375, ((0, 8),)),
        "inter_embed": gaussian(key_of[4], (VOCAB, M), 1.0, 4.0, ((1, 8),)),
        "gate_weight": gaussian(key_of[5], (M, GATES), (M // 4) ** -0.5, 0.1875, ((1, 8),)),
        "gate_embed": gaussian(key_of[6], (VOCAB, GATES), 0.5, 3.0, ((1, 8),)),
        "gate_bias": gaussian(key_of[7], (GATES,), 0.5, 3.0, ((0, 8),), jnp.float32),
    }


def reference(byte_ids, h_start, c_start, inter_weight, inter_embed, gate_weight, gate_embed, gate_bias):
    hidden = h_start
    cell_state = c_start
    streams_here = h_start.shape[0]
    for step in range(STEPS):
        onehot = (byte_ids[step][:, None] == jnp.arange(VOCAB, dtype=jnp.int32)[None, :]).astype(jnp.bfloat16)
        product = lax.dot_general(hidden, inter_weight, (((1,), (1,)), ((), ())), preferred_element_type=jnp.float32)
        lookup = jnp.dot(onehot, inter_embed, preferred_element_type=jnp.float32)
        inter_vals = (lookup * product).astype(jnp.bfloat16)
        gate_sums = jnp.dot(inter_vals, gate_weight, preferred_element_type=jnp.float32)
        gate_sums = gate_sums + jnp.dot(onehot, gate_embed, preferred_element_type=jnp.float32) + gate_bias[None, :]
        gate_sums = gate_sums.reshape(streams_here, H, 4)
        in_gate = jax.nn.sigmoid(gate_sums[:, :, 0])
        forget = jax.nn.sigmoid(gate_sums[:, :, 1])
        out_gate = jax.nn.sigmoid(gate_sums[:, :, 2])
        update = jnp.tanh(gate_sums[:, :, 3])
        cell_state = forget * cell_state + in_gate * update
        hidden = (out_gate * jnp.tanh(cell_state)).astype(jnp.bfloat16)
    return hidden, cell_state
```

```python
import jax
import jax.numpy as jnp
from jax import lax
from jax.experimental import pallas as pl
from jax.experimental.pallas import tpu as pltpu
from jax.sharding import PartitionSpec as P

GATE_KINDS = 4
LANES = 128
MAX_RING = 8


def plain(
    byte_ids, h_start, c_start, inter_weight, inter_embed, gate_weight, gate_embed, gate_bias
):
    hidden = h_start
    cell = c_start
    for step in range(byte_ids.shape[0]):
        rows_here = hidden.shape[0]
        onehot = one_hot(byte_ids[step], inter_embed.shape[0])
        product = lax.dot_general(
            lax.all_gather(hidden, "mp", axis=1, tiled=True),
            inter_weight,
            (((1,), (1,)), ((), ())),
            preferred_element_type=jnp.float32,
        )
        lookup = jnp.dot(onehot, inter_embed, preferred_element_type=jnp.float32)
        inter_vals = (lookup * product).astype(jnp.bfloat16)
        gate_sums = jnp.dot(
            lax.all_gather(inter_vals, "mp", axis=1, tiled=True),
            gate_weight,
            preferred_element_type=jnp.float32,
        )
        gate_sums = (
            gate_sums
            + jnp.dot(onehot, gate_embed, preferred_element_type=jnp.float32)
            + gate_bias[None, :]
        )
        gate_sums = gate_sums.reshape(rows_here, gate_sums.shape[1] // GATE_KINDS, GATE_KINDS)
        hidden, cell = update_state([gate_sums[:, :, j] for j in range(GATE_KINDS)], cell)
    return hidden, cell


def one_hot(ids, vocab):
    return (ids[:, None] == jnp.arange(vocab, dtype=jnp.int32)[None, :]).astype(jnp.bfloat16)


def update_state(sums, cell):
    in_gate = jax.nn.sigmoid(sums[0])
    forget = jax.nn.sigmoid(sums[1])
    out_gate = jax.nn.sigmoid(sums[2])
    update = jnp.tanh(sums[3])
    cell = forget * cell + in_gate * update
    return (out_gate * jnp.tanh(cell)).astype(jnp.bfloat16), cell


def by_gate_kernel(order_ref, embed_ref, weight_ref, out_ref, mix_ref):
    group = GATE_KINDS * LANES
    units = out_ref.shape[1] // GATE_KINDS

    @pl.when(pl.program_id(0) == 0)
    def _():
        source = lax.broadcasted_iota(jnp.int32, (group, group), 0)
        target = lax.broadcasted_iota(jnp.int32, (group, group), 1)
        wanted = (target % LANES) * GATE_KINDS + target // LANES
        mix_ref[...] = (source == wanted).astype(jnp.float32).astype(jnp.bfloat16)

    def write(block_ref):
        for g in range(units // LANES):
            mixed = jnp.dot(
                block_ref[:, g * group : (g + 1) * group],
                mix_ref[...],
                preferred_element_type=jnp.float32,
            ).astype(jnp.bfloat16)
            for j in range(GATE_KINDS):
                out_ref[:, j * units + g * LANES : j * units + (g + 1) * LANES] = mixed[
                    :, j * LANES : (j + 1) * LANES
                ]

    @pl.when(pl.program_id(0) == 0)
    def _():
        write(embed_ref)

    @pl.when(pl.program_id(0) > 0)
    def _():
        write(weight_ref)


def by_gate(order, gate_embed, gate_weight, part):
    rows, columns = gate_embed.shape
    each = part // rows
    group = GATE_KINDS * LANES

    def weight_at(i, order_ref):
        k = jnp.maximum(i - 1, 0)
        return order_ref[k // each] * each + k % each, 0

    return pl.pallas_call(
        by_gate_kernel,
        grid_spec=pltpu.PrefetchScalarGridSpec(
            num_scalar_prefetch=1,
            grid=(1 + gate_weight.shape[0] // rows,),
            in_specs=[
                pl.BlockSpec((rows, columns), lambda i, order_ref: (0, 0)),
                pl.BlockSpec((rows, columns), weight_at),
            ],
            out_specs=pl.BlockSpec((rows, columns), lambda i, order_ref: (i, 0)),
            scratch_shapes=[pltpu.VMEM((group, group), jnp.bfloat16)],
        ),
        out_shape=jax.ShapeDtypeStruct((rows + gate_weight.shape[0], columns), jnp.bfloat16),
        compiler_params=pltpu.CompilerParams(vmem_limit_bytes=32 * 2**20),
        cost_estimate=pl.CostEstimate(
            flops=2 * (rows + gate_weight.shape[0]) * columns * group,
            bytes_accessed=4 * (rows + gate_weight.shape[0]) * columns,
            transcendentals=0,
        ),
    )(order, gate_embed, gate_weight)


def turn_kernel(order_ref, weight_ref, out_ref):
    out_ref[...] = weight_ref[...].T


def turned(order, inter_weight, part):
    rows, columns = inter_weight.shape
    return pl.pallas_call(
        turn_kernel,
        grid_spec=pltpu.PrefetchScalarGridSpec(
            num_scalar_prefetch=1,
            grid=(columns // part,),
            in_specs=[pl.BlockSpec((rows, part), lambda i, order_ref: (0, order_ref[i]))],
            out_specs=pl.BlockSpec((part, rows), lambda i, order_ref: (i, 0)),
        ),
        out_shape=jax.ShapeDtypeStruct((columns, rows), jnp.bfloat16),
        compiler_params=pltpu.CompilerParams(vmem_limit_bytes=32 * 2**20),
        cost_estimate=pl.CostEstimate(
            flops=0, bytes_accessed=4 * rows * columns, transcendentals=0
        ),
    )(order, inter_weight)


def ring_of(devices):
    return list(range(0, devices, 2)) + list(range(devices - 1, 0, -2))


def arrivals(block, ring, last_up):
    devices = len(ring)
    up = [(ring[i], ring[(i + 1) % devices]) for i in range(devices)]
    down = [(b, a) for a, b in up]
    groups = [[block]]
    from_below = from_above = block
    for _ in range(devices // 2 - 1):
        from_below = lax.ppermute(from_below, "mp", up)
        from_above = lax.ppermute(from_above, "mp", down)
        groups.append([from_below, from_above])
    groups.append(
        [lax.ppermute(from_below, "mp", up) if last_up else lax.ppermute(from_above, "mp", down)]
    )
    return groups


def gathered_dot(groups, weight, total=None, first=None):
    at = 0
    for index, group in enumerate(groups):
        parts = list(group)
        if index == 0 and first is not None:
            parts = [first] + parts
        for part in parts:
            term = jnp.dot(
                part, weight[at : at + part.shape[1]], preferred_element_type=jnp.float32
            )
            total = term if total is None else total + term
            at += part.shape[1]
    return total


def ringed(devices, chunks):
    ring = ring_of(devices)
    place = [ring.index(i) for i in range(devices)]

    def local(
        byte_ids, h_start, c_start, inter_weight, inter_embed, gate_weight, gate_embed, gate_bias
    ):
        part = h_start.shape[1]
        here = jnp.array(place, jnp.int32)[lax.axis_index("mp")]
        steps_away = [0]
        for k in range(1, devices // 2):
            steps_away += [-k, k]
        steps_away.append(devices // 2)
        order = jnp.array(ring, jnp.int32)[
            (here + jnp.array(steps_away, jnp.int32) + devices) % devices
        ]
        weight_in = turned(order, inter_weight, part)
        weight_gate = by_gate(order, gate_embed, gate_weight, part)
        bias = gate_bias.reshape(-1, GATE_KINDS).T.reshape(1, -1)
        vocab = inter_embed.shape[0]
        rows = h_start.shape[0] // chunks
        hidden = [h_start[c * rows : (c + 1) * rows] for c in range(chunks)]
        cell = [c_start[c * rows : (c + 1) * rows] for c in range(chunks)]
        for step in range(byte_ids.shape[0]):
            for c in range(chunks):
                onehot = one_hot(byte_ids[step, c * rows : (c + 1) * rows], vocab)
                lookup = jnp.dot(onehot, inter_embed, preferred_element_type=jnp.float32)
                product = gathered_dot(arrivals(hidden[c], ring, c % 2 == 0), weight_in)
                inter = (lookup * product).astype(jnp.bfloat16)
                sums = gathered_dot(
                    arrivals(inter, ring, c % 2 == 0), weight_gate, first=onehot
                )
                sums = sums + bias
                hidden[c], cell[c] = update_state(
                    [sums[:, j * part : (j + 1) * part] for j in range(GATE_KINDS)], cell[c]
                )
        return jnp.concatenate(hidden, 0), jnp.concatenate(cell, 0)

    return local


def solution(mesh):
    in_specs = (
        P(None, ("groups", "batch")),
        P(("groups", "batch"), "mp"),
        P(("groups", "batch"), "mp"),
        P("mp", None),
        P(None, "mp"),
        P(None, "mp"),
        P(None, "mp"),
        P("mp"),
    )
    out_specs = (P(("groups", "batch"), "mp"), P(("groups", "batch"), "mp"))
    devices = mesh.shape["mp"]
    local = ringed(devices, 2) if 2 < devices <= MAX_RING else plain
    return jax.shard_map(local, mesh=mesh, in_specs=in_specs, out_specs=out_specs, check_vma=False)
```

```python
import jax
import jax.numpy as jnp
from jax import lax
from jax.experimental import pallas as pl
from jax.experimental.pallas import tpu as pltpu
from jax.sharding import PartitionSpec as P

GATE_KINDS = 4
LANES = 128
MAX_RING = 8


def plain(
    byte_ids, h_start, c_start, inter_weight, inter_embed, gate_weight, gate_embed, gate_bias
):
    hidden = h_start
    cell = c_start
    for step in range(byte_ids.shape[0]):
        rows_here = hidden.shape[0]
        onehot = one_hot(byte_ids[step], inter_embed.shape[0])
        product = lax.dot_general(
            lax.all_gather(hidden, "mp", axis=1, tiled=True),
            inter_weight,
            (((1,), (1,)), ((), ())),
            preferred_element_type=jnp.float32,
        )
        lookup = jnp.dot(onehot, inter_embed, preferred_element_type=jnp.float32)
        inter_vals = (lookup * product).astype(jnp.bfloat16)
        gate_sums = jnp.dot(
            lax.all_gather(inter_vals, "mp", axis=1, tiled=True),
            gate_weight,
            preferred_element_type=jnp.float32,
        )
        gate_sums = (
            gate_sums
            + jnp.dot(onehot, gate_embed, preferred_element_type=jnp.float32)
            + gate_bias[None, :]
        )
        gate_sums = gate_sums.reshape(rows_here, gate_sums.shape[1] // GATE_KINDS, GATE_KINDS)
        hidden, cell = update_state([gate_sums[:, :, j] for j in range(GATE_KINDS)], cell)
    return hidden, cell


def one_hot(ids, vocab):
    return (ids[:, None] == jnp.arange(vocab, dtype=jnp.int32)[None, :]).astype(jnp.bfloat16)


def update_state(sums, cell):
    in_gate = jax.nn.sigmoid(sums[0])
    forget = jax.nn.sigmoid(sums[1])
    out_gate = jax.nn.sigmoid(sums[2])
    update = jnp.tanh(sums[3])
    cell = forget * cell + in_gate * update
    return (out_gate * jnp.tanh(cell)).astype(jnp.bfloat16), cell


def ring_of(devices):
    return list(range(0, devices, 2)) + list(range(devices - 1, 0, -2))


def ring_index(me, steps, devices):
    place = jnp.where(me % 2 == 0, me // 2, devices - 1 - me // 2)
    place = (place + steps + devices) % devices
    half = devices // 2
    return jnp.where(place < half, 2 * place, 2 * (devices - 1 - place) + 1)


def mix_into(mix_ref):
    group = mix_ref.shape[0]
    lanes = group // GATE_KINDS
    source = lax.broadcasted_iota(jnp.int32, (group, group), 0)
    target = lax.broadcasted_iota(jnp.int32, (group, group), 1)
    wanted = (target % lanes) * GATE_KINDS + target // lanes
    mix_ref[...] = (source == wanted).astype(jnp.float32).astype(jnp.bfloat16)


def sort_columns(block, mix, out_ref):
    group = mix.shape[0]
    lanes = group // GATE_KINDS
    units = out_ref.shape[1] // GATE_KINDS
    for g in range(units // lanes):
        mixed = jnp.dot(
            block[:, g * group : (g + 1) * group], mix, preferred_element_type=jnp.float32
        ).astype(out_ref.dtype)
        for j in range(GATE_KINDS):
            to = j * units + g * lanes
            out_ref[:, to : to + lanes] = mixed[:, j * lanes : (j + 1) * lanes]


def embed_kernel(embed_ref, bias_ref, out_ref, bias_out_ref, mix_ref):
    mix_into(mix_ref)
    sort_columns(embed_ref[...], mix_ref[...], out_ref)
    bias = jnp.broadcast_to(bias_ref[...], bias_out_ref.shape)
    high = bias.astype(jnp.bfloat16)
    left = bias - high.astype(jnp.float32)
    middle = left.astype(jnp.bfloat16)
    low = (left - middle.astype(jnp.float32)).astype(jnp.bfloat16)
    group = mix_ref.shape[0]
    lanes = group // GATE_KINDS
    units = out_ref.shape[1] // GATE_KINDS
    for g in range(units // lanes):
        here = slice(g * group, (g + 1) * group)
        mixed = [
            jnp.dot(term[:, here], mix_ref[...], preferred_element_type=jnp.float32)
            for term in (high, middle, low)
        ]
        mixed = (mixed[0] + mixed[1]) + mixed[2]
        for j in range(GATE_KINDS):
            to = j * units + g * lanes
            bias_out_ref[:, to : to + lanes] = mixed[:, j * lanes : (j + 1) * lanes]


def embed_by_gate(gate_embed, gate_bias):
    rows, columns = gate_embed.shape
    group = GATE_KINDS * LANES
    return pl.pallas_call(
        embed_kernel,
        out_shape=(
            jax.ShapeDtypeStruct((rows, columns), jnp.bfloat16),
            jax.ShapeDtypeStruct((8, columns), jnp.float32),
        ),
        scratch_shapes=[pltpu.VMEM((group, group), jnp.bfloat16)],
        compiler_params=pltpu.CompilerParams(vmem_limit_bytes=12 * 2**20),
        cost_estimate=pl.CostEstimate(
            flops=2 * rows * columns * group, bytes_accessed=4 * rows * columns, transcendentals=0
        ),
    )(gate_embed, gate_bias.reshape(1, columns))


def weight_kernel(me_ref, weight_ref, after_ref, out_ref, mix_ref):
    @pl.when(pl.program_id(0) == 0)
    def _():
        mix_into(mix_ref)

    sort_columns(weight_ref[...], mix_ref[...], out_ref)


def weight_by_gate(me, gate_weight, part, steps, devices, after):
    columns = gate_weight.shape[1]
    group = GATE_KINDS * LANES

    def block_at(i, me_ref):
        away = steps[0]
        for k in range(1, len(steps)):
            away = jnp.where(i == k, steps[k], away)
        return ring_index(me_ref[0], away, devices), 0

    return pl.pallas_call(
        weight_kernel,
        grid_spec=pltpu.PrefetchScalarGridSpec(
            num_scalar_prefetch=1,
            grid=(len(steps),),
            in_specs=[
                pl.BlockSpec((part, columns), block_at),
                pl.BlockSpec(memory_space=pl.ANY),
            ],
            out_specs=pl.BlockSpec((part, columns), lambda i, me_ref: (i, 0)),
            scratch_shapes=[pltpu.VMEM((group, group), jnp.bfloat16)],
        ),
        out_shape=jax.ShapeDtypeStruct((len(steps) * part, columns), jnp.bfloat16),
        compiler_params=pltpu.CompilerParams(vmem_limit_bytes=14 * 2**20),
        cost_estimate=pl.CostEstimate(
            flops=2 * len(steps) * part * columns * group,
            bytes_accessed=4 * len(steps) * part * columns,
            transcendentals=0,
        ),
    )(me, gate_weight, after)


def turn_kernel(me_ref, weight_ref, out_ref):
    out_ref[...] = weight_ref[...].T


def turned(me, inter_weight, part, away, devices):
    rows, columns = inter_weight.shape

    def block_at(i, me_ref):
        steps = jnp.where(i % 2 == 1, -((i + 1) // 2), i // 2)
        return 0, ring_index(me_ref[0], steps, devices)

    assert away == [(-((i + 1) // 2) if i % 2 else i // 2) % devices for i in range(devices)]
    return pl.pallas_call(
        turn_kernel,
        grid_spec=pltpu.PrefetchScalarGridSpec(
            num_scalar_prefetch=1,
            grid=(columns // part,),
            in_specs=[pl.BlockSpec((rows, part), block_at)],
            out_specs=pl.BlockSpec((part, rows), lambda i, me_ref: (i, 0)),
        ),
        out_shape=jax.ShapeDtypeStruct((columns, rows), jnp.bfloat16),
        compiler_params=pltpu.CompilerParams(vmem_limit_bytes=8 * 2**20),
        cost_estimate=pl.CostEstimate(
            flops=0, bytes_accessed=4 * rows * columns, transcendentals=0
        ),
    )(me, inter_weight)


def arrivals(block, ring, last):
    devices = len(ring)
    up = [(ring[i], ring[(i + 1) % devices]) for i in range(devices)]
    down = [(b, a) for a, b in up]
    groups = [[block]]
    below = above = block
    for _ in range(devices // 2 - 1):
        below = lax.ppermute(below, "mp", up)
        above = lax.ppermute(above, "mp", down)
        groups.append([below, above])
    if last == "up":
        farthest = lax.ppermute(below, "mp", up)
    elif last == "down":
        farthest = lax.ppermute(above, "mp", down)
    else:
        half = block.shape[0] // 2
        farthest = jnp.concatenate(
            [lax.ppermute(below[:half], "mp", up), lax.ppermute(above[half:], "mp", down)], 0
        )
    return groups + [[farthest]]


def dot32(a, b):
    return jnp.dot(a, b, preferred_element_type=jnp.float32)


def gathered_dot(arrived, weights, total=None):
    for k in range(len(weights) - 1):
        block = jnp.concatenate([jnp.concatenate(groups[k], 1) for groups in arrived], 0)
        term = dot32(block, weights[k])
        total = term if total is None else total + term
    rows = arrived[0][0][0].shape[0]
    return [
        total[c * rows : (c + 1) * rows] + dot32(groups[-1][0], weights[-1])
        for c, groups in enumerate(arrived)
    ]


def ringed(devices, chunks):
    ring = ring_of(devices)
    groups_away = [[0]] + [[-k, k] for k in range(1, devices // 2)] + [[devices // 2]]

    def local(
        byte_ids, h_start, c_start, inter_weight, inter_embed, gate_weight, gate_embed, gate_bias
    ):
        steps, streams = byte_ids.shape
        part = h_start.shape[1]
        rows = streams // chunks
        me = jnp.full((1,), lax.axis_index("mp"), jnp.int32)
        arrived = [arrivals(h_start, ring, "both")]
        weight_in = turned(
            me, inter_weight, part, [a % devices for g in groups_away for a in g], devices
        )
        ends = [0]
        for away in groups_away:
            ends.append(ends[-1] + len(away) * part)
        weights_in = [weight_in[ends[k] : ends[k + 1]] for k in range(len(groups_away))]
        embed, bias = embed_by_gate(gate_embed, gate_bias)
        weights_gate = [
            weight_by_gate(me, gate_weight, part, away, devices, arrived[0][min(k + 1, len(groups_away) - 1)][-1])
            for k, away in enumerate(groups_away)
        ]
        onehot = one_hot(byte_ids.reshape(-1), inter_embed.shape[0])
        lookup = dot32(onehot, inter_embed).astype(jnp.bfloat16)
        cells = [c_start[c * rows : (c + 1) * rows] for c in range(chunks)]
        ways = ["up" if c % 2 == 0 else "down" for c in range(chunks)] if chunks > 1 else ["both"]
        for step in range(steps):
            at = step * streams
            products = gathered_dot(arrived, weights_in)
            if len(products) < chunks:
                products = [products[0][c * rows : (c + 1) * rows] for c in range(chunks)]
            inters = [
                (lookup[at + c * rows : at + (c + 1) * rows].astype(jnp.float32) * product).astype(
                    jnp.bfloat16
                )
                for c, product in enumerate(products)
            ]
            arrived = [arrivals(inter, ring, way) for inter, way in zip(inters, ways)]
            sums = gathered_dot(arrived, weights_gate, dot32(onehot[at : at + streams], embed))
            hiddens = []
            for c in range(chunks):
                full = sums[c] + bias[:1]
                hidden, cells[c] = update_state(
                    [full[:, j * part : (j + 1) * part] for j in range(GATE_KINDS)], cells[c]
                )
                hiddens.append(hidden)
            if step + 1 < steps:
                arrived = [arrivals(hidden, ring, way) for hidden, way in zip(hiddens, ways)]
        return jnp.concatenate(hiddens, 0), jnp.concatenate(cells, 0)

    return local


def solution(mesh):
    in_specs = (
        P(None, ("groups", "batch")),
        P(("groups", "batch"), "mp"),
        P(("groups", "batch"), "mp"),
        P("mp", None),
        P(None, "mp"),
        P(None, "mp"),
        P(None, "mp"),
        P("mp"),
    )
    out_specs = (P(("groups", "batch"), "mp"), P(("groups", "batch"), "mp"))
    devices = mesh.shape["mp"]
    local = ringed(devices, 2) if 2 < devices <= MAX_RING else plain
    return jax.shard_map(local, mesh=mesh, in_specs=in_specs, out_specs=out_specs, check_vma=False)
```

```python
import math

import jax
import jax.numpy as jnp
from jax import lax
from jax.experimental import pallas as pl
from jax.experimental.pallas import tpu as pltpu
from jax.sharding import PartitionSpec as P

GATE_KINDS = 4
LANES = 128
MAX_RING = 8
SCRATCH = 16 * 2**20


def plain(
    byte_ids, h_start, c_start, inter_weight, inter_embed, gate_weight, gate_embed, gate_bias
):
    hidden = h_start
    cell = c_start
    for step in range(byte_ids.shape[0]):
        rows_here = hidden.shape[0]
        onehot = one_hot(byte_ids[step], inter_embed.shape[0])
        product = lax.dot_general(
            lax.all_gather(hidden, "mp", axis=1, tiled=True),
            inter_weight,
            (((1,), (1,)), ((), ())),
            preferred_element_type=jnp.float32,
        )
        lookup = jnp.dot(onehot, inter_embed, preferred_element_type=jnp.float32)
        inter_vals = (lookup * product).astype(jnp.bfloat16)
        gate_sums = jnp.dot(
            lax.all_gather(inter_vals, "mp", axis=1, tiled=True),
            gate_weight,
            preferred_element_type=jnp.float32,
        )
        gate_sums = (
            gate_sums
            + jnp.dot(onehot, gate_embed, preferred_element_type=jnp.float32)
            + gate_bias[None, :]
        )
        gate_sums = gate_sums.reshape(rows_here, gate_sums.shape[1] // GATE_KINDS, GATE_KINDS)
        hidden, cell = update_state([gate_sums[:, :, j] for j in range(GATE_KINDS)], cell)
    return hidden, cell


def one_hot(ids, vocab):
    return (ids[:, None] == jnp.arange(vocab, dtype=jnp.int32)[None, :]).astype(jnp.bfloat16)


def update_state(sums, cell):
    in_gate = jax.nn.sigmoid(sums[0])
    forget = jax.nn.sigmoid(sums[1])
    out_gate = jax.nn.sigmoid(sums[2])
    update = jnp.tanh(sums[3])
    cell = forget * cell + in_gate * update
    return (out_gate * jnp.tanh(cell)).astype(jnp.bfloat16), cell


def ring_of(devices):
    return list(range(0, devices, 2)) + list(range(devices - 1, 0, -2))


def ring_index(me, steps, devices):
    place = jnp.where(me % 2 == 0, me // 2, devices - 1 - me // 2)
    place = (place + steps + devices) % devices
    half = devices // 2
    return jnp.where(place < half, 2 * place, 2 * (devices - 1 - place) + 1)


def mix_matrix(group):
    lanes = group // GATE_KINDS
    source = jnp.arange(group, dtype=jnp.int32)[:, None]
    target = jnp.arange(group, dtype=jnp.int32)[None, :]
    wanted = (target % lanes) * GATE_KINDS + target // lanes
    return (source == wanted).astype(jnp.bfloat16)


def dot32(a, b):
    return jnp.dot(a, b, preferred_element_type=jnp.float32)


def dot32_turned(a, b):
    return lax.dot_general(a, b, (((1,), (1,)), ((), ())), preferred_element_type=jnp.float32)


def rows_of(refs):
    blocks = [ref[...] for ref in refs]
    return blocks[0] if len(blocks) == 1 else jnp.concatenate(blocks, 0)


class Gather:
    def __init__(self, me, weight, devices, part, turned):
        self.me, self.weight = me, weight
        self.devices, self.part, self.turned = devices, part, turned
        self.columns = weight.shape[0] if turned else weight.shape[1]

    def terms(self, me_ref, weight_ref, blocks, away, columns):
        total = None
        for block, steps in zip(blocks, away):
            start = pl.multiple_of(
                ring_index(me_ref[0], steps, self.devices) * self.part, self.part
            )
            if self.turned:
                term = dot32_turned(block, weight_ref[columns, pl.ds(start, self.part)])
            else:
                term = dot32(block, weight_ref[pl.ds(start, self.part), columns])
            total = term if total is None else total + term
        return total

    def tiles(self):
        width = min(self.columns, GATE_KINDS * LANES)
        return [slice(at, at + width) for at in range(0, self.columns, width)]

    def add(self, groups, away, total=None, first=None):
        chunks = len(groups[0])
        rows = sum(block.shape[0] for block in groups[0])
        extra = [] if total is None else [total]
        at = 0
        if first is not None:
            onehot, at, embed = first
            extra = [onehot, embed]

        def kernel(me_ref, weight_ref, *refs):
            extra_refs, refs, out_ref = refs[: len(extra)], refs[len(extra) : -1], refs[-1]
            blocks = [rows_of(refs[i * chunks : (i + 1) * chunks]) for i in range(len(away))]
            for columns in self.tiles():
                value = self.terms(me_ref, weight_ref, blocks, away, columns)
                if total is not None:
                    value = extra_refs[0][:, columns] + value
                if first is not None:
                    value = dot32(extra_refs[0][at : at + rows], extra_refs[1][:, columns]) + value
                out_ref[:, columns] = value

        return call(
            kernel,
            [self.me, self.weight, *extra, *[block for group in groups for block in group]],
            [jax.ShapeDtypeStruct((rows, self.columns), jnp.float32)],
            2 * rows * self.columns * self.part * len(away),
        )[0]


def call(kernel, operands, outs, flops):
    size = sum(math.prod(out.shape) * out.dtype.itemsize for out in outs)
    return pl.pallas_call(
        kernel,
        in_specs=[pl.BlockSpec(memory_space=pltpu.SMEM)]
        + [pl.BlockSpec(memory_space=pltpu.VMEM)] * (len(operands) - 1),
        out_specs=[pl.BlockSpec(memory_space=pltpu.VMEM)] * len(outs),
        out_shape=outs,
        compiler_params=pltpu.CompilerParams(vmem_limit_bytes=SCRATCH),
        cost_estimate=pl.CostEstimate(flops=flops, bytes_accessed=size, transcendentals=0),
    )(*operands)


def inter_of(gather, total, last, row, onehot, at, inter_embed, away):
    rows = last.shape[0]

    def kernel(me_ref, weight_ref, total_ref, last_ref, onehot_ref, embed_ref, out_ref):
        product = total_ref[row : row + rows] + gather.terms(
            me_ref, weight_ref, [last_ref[...]], [away], slice(None)
        )
        lookup = dot32(onehot_ref[at + row : at + row + rows], embed_ref[...])
        out_ref[...] = (lookup * product).astype(out_ref.dtype)

    return call(
        kernel,
        [gather.me, gather.weight, total, last, onehot, inter_embed],
        [jax.ShapeDtypeStruct((rows, gather.columns), jnp.bfloat16)],
        2 * rows * gather.columns * gather.part,
    )[0]


def state_of(gather, total, lasts, row, bias, cell, cell_row, mix, away):
    rows = sum(last.shape[0] for last in lasts)
    group = mix.shape[0]
    lanes = group // GATE_KINDS
    units = gather.columns // GATE_KINDS
    chunks = len(lasts)

    def kernel(me_ref, weight_ref, total_ref, bias_ref, cell_ref, mix_ref, *refs):
        last_refs, hidden_ref, cell_out_ref = refs[:chunks], refs[chunks], refs[chunks + 1]
        last = rows_of(last_refs)
        terms = []
        for columns in gather.tiles():
            full = total_ref[row : row + rows, columns] + gather.terms(
                me_ref, weight_ref, [last], [away], columns
            )
            full = full + bias_ref[:, columns]
            high = full.astype(jnp.bfloat16)
            terms += [high, (full - high.astype(jnp.float32)).astype(jnp.bfloat16)]
        mixed = dot32(jnp.concatenate(terms, 0), mix_ref[...])
        for g in range(len(terms) // 2):
            at = 2 * g * rows
            sums = mixed[at : at + rows] + mixed[at + rows : at + 2 * rows]
            here = slice(g * lanes, (g + 1) * lanes)
            hidden_ref[:, here], cell_out_ref[:, here] = update_state(
                [sums[:, j * lanes : (j + 1) * lanes] for j in range(GATE_KINDS)],
                cell_ref[cell_row : cell_row + rows, here],
            )

    return call(
        kernel,
        [gather.me, gather.weight, total, bias, cell, mix, *lasts],
        [
            jax.ShapeDtypeStruct((rows, units), jnp.bfloat16),
            jax.ShapeDtypeStruct((rows, units), jnp.float32),
        ],
        2 * rows * gather.columns * (gather.part + 2 * group),
    )


def arrivals(block, ring, last):
    devices = len(ring)
    up = [(ring[i], ring[(i + 1) % devices]) for i in range(devices)]
    down = [(b, a) for a, b in up]
    blocks = [block]
    below = above = block
    for _ in range(devices // 2 - 1):
        below = lax.ppermute(below, "mp", up)
        above = lax.ppermute(above, "mp", down)
        blocks += [below, above]
    if last == "up":
        farthest = [lax.ppermute(below, "mp", up)]
    elif last == "down":
        farthest = [lax.ppermute(above, "mp", down)]
    else:
        half = block.shape[0] // 2
        farthest = [
            lax.ppermute(below[:half], "mp", up),
            lax.ppermute(above[half:], "mp", down),
        ]
    return blocks, farthest


def ringed(devices, chunks, first_chunks):
    ring = ring_of(devices)
    away = [-((k + 1) // 2) if k % 2 else k // 2 for k in range(devices)]

    def local(
        byte_ids, h_start, c_start, inter_weight, inter_embed, gate_weight, gate_embed, gate_bias
    ):
        steps, streams = byte_ids.shape
        part = h_start.shape[1]
        me = jnp.full((1,), lax.axis_index("mp"), jnp.int32)
        to_inter = Gather(me, inter_weight, devices, part, True)
        to_gate = Gather(me, gate_weight, devices, part, False)
        mix = mix_matrix(GATE_KINDS * LANES)
        bias = gate_bias.reshape(1, -1)
        onehot = one_hot(byte_ids.reshape(-1), inter_embed.shape[0])

        def gathered(blocks, gather, first=None):
            ways = ["up" if c % 2 == 0 else "down" for c in range(len(blocks))]
            if len(blocks) == 1:
                ways = ["both"]
            arrived, farthest = zip(*[arrivals(b, ring, way) for b, way in zip(blocks, ways)])
            total = gather.add([[b[0] for b in arrived]], away[:1], first=first)
            for k in range(1, devices - 1, 2):
                total = gather.add(
                    [[b[k] for b in arrived], [b[k + 1] for b in arrived]],
                    away[k : k + 2],
                    total,
                )
            return total, [last for lasts in farthest for last in lasts]

        rows = streams // first_chunks
        hiddens = [h_start[c * rows : (c + 1) * rows] for c in range(first_chunks)]
        rows = streams // chunks
        cells = [(c_start, c * rows) for c in range(chunks)]
        for step in range(steps):
            at = step * streams
            total, lasts = gathered(hiddens, to_inter)
            inters = [
                inter_of(to_inter, total, last, c * rows, onehot, at, inter_embed, away[-1])
                for c, last in enumerate(lasts)
            ]
            total, lasts = gathered(inters, to_gate, (onehot, at, gate_embed))
            if step + 1 < steps:
                hiddens, updated = zip(
                    *[
                        state_of(to_gate, total, [last], c * rows, bias, *cells[c], mix, away[-1])
                        for c, last in enumerate(lasts)
                    ]
                )
                cells = [(cell, 0) for cell in updated]
            else:
                cell = cells[0][0]
                if cell.shape[0] < streams:
                    cell = jnp.concatenate([cell for cell, _ in cells], 0)
                return state_of(to_gate, total, lasts, 0, bias, cell, 0, mix, away[-1])

    return local


def solution(mesh):
    in_specs = (
        P(None, ("groups", "batch")),
        P(("groups", "batch"), "mp"),
        P(("groups", "batch"), "mp"),
        P("mp", None),
        P(None, "mp"),
        P(None, "mp"),
        P(None, "mp"),
        P("mp"),
    )
    out_specs = (P(("groups", "batch"), "mp"), P(("groups", "batch"), "mp"))
    devices = mesh.shape["mp"]
    local = ringed(devices, 2, 1) if 2 < devices <= MAX_RING else plain
    return jax.shard_map(local, mesh=mesh, in_specs=in_specs, out_specs=out_specs, check_vma=False)
```

```python
import math

import jax
import jax.numpy as jnp
from jax import lax
from jax.experimental import pallas as pl
from jax.experimental.pallas import tpu as pltpu
from jax.sharding import PartitionSpec as P

GATE_KINDS = 4
LANES = 128
MAX_RING = 8
SCRATCH = 16 * 2**20


def plain(
    byte_ids, h_start, c_start, inter_weight, inter_embed, gate_weight, gate_embed, gate_bias
):
    hidden = h_start
    cell = c_start
    for step in range(byte_ids.shape[0]):
        rows_here = hidden.shape[0]
        onehot = one_hot(byte_ids[step], inter_embed.shape[0])
        product = lax.dot_general(
            lax.all_gather(hidden, "mp", axis=1, tiled=True),
            inter_weight,
            (((1,), (1,)), ((), ())),
            preferred_element_type=jnp.float32,
        )
        lookup = jnp.dot(onehot, inter_embed, preferred_element_type=jnp.float32)
        inter_vals = (lookup * product).astype(jnp.bfloat16)
        gate_sums = jnp.dot(
            lax.all_gather(inter_vals, "mp", axis=1, tiled=True),
            gate_weight,
            preferred_element_type=jnp.float32,
        )
        gate_sums = (
            gate_sums
            + jnp.dot(onehot, gate_embed, preferred_element_type=jnp.float32)
            + gate_bias[None, :]
        )
        gate_sums = gate_sums.reshape(rows_here, gate_sums.shape[1] // GATE_KINDS, GATE_KINDS)
        hidden, cell = update_state([gate_sums[:, :, j] for j in range(GATE_KINDS)], cell)
    return hidden, cell


def one_hot(ids, vocab):
    return (ids[..., None] == jnp.arange(vocab, dtype=jnp.int32)).astype(jnp.bfloat16)


def update_state(sums, cell):
    in_gate = jax.nn.sigmoid(sums[0])
    forget = jax.nn.sigmoid(sums[1])
    out_gate = jax.nn.sigmoid(sums[2])
    update = jnp.tanh(sums[3])
    cell = forget * cell + in_gate * update
    return (out_gate * jnp.tanh(cell)).astype(jnp.bfloat16), cell


def ring_of(devices):
    return list(range(0, devices, 2)) + list(range(devices - 1, 0, -2))


def ring_index(me, steps, devices):
    place = jnp.where(me % 2 == 0, me // 2, devices - 1 - me // 2)
    place = (place + steps + devices) % devices
    half = devices // 2
    return jnp.where(place < half, 2 * place, 2 * (devices - 1 - place) + 1)


def mix_matrix(group):
    lanes = group // GATE_KINDS
    source = jnp.arange(group, dtype=jnp.int32)[:, None]
    target = jnp.arange(group, dtype=jnp.int32)[None, :]
    wanted = (target % lanes) * GATE_KINDS + target // lanes
    return (source == wanted).astype(jnp.bfloat16)


def dot32(a, b):
    return jnp.dot(a, b, preferred_element_type=jnp.float32)


def dot32_turned(a, b):
    return lax.dot_general(a, b, (((1,), (1,)), ((), ())), preferred_element_type=jnp.float32)


def rows_of(refs):
    blocks = [ref[...] for ref in refs]
    return blocks[0] if len(blocks) == 1 else jnp.concatenate(blocks, 0)


class Gather:
    def __init__(self, me, weight, devices, part, turned):
        self.me, self.weight = me, weight
        self.devices, self.part, self.turned = devices, part, turned
        self.columns = weight.shape[0] if turned else weight.shape[1]

    def terms(self, me_ref, weight_ref, blocks, away, columns):
        total = None
        for block, steps in zip(blocks, away):
            start = pl.multiple_of(
                ring_index(me_ref[0], steps, self.devices) * self.part, self.part
            )
            if self.turned:
                term = dot32_turned(block, weight_ref[columns, pl.ds(start, self.part)])
            else:
                term = dot32(block, weight_ref[pl.ds(start, self.part), columns])
            total = term if total is None else total + term
        return total

    def tiles(self):
        width = min(self.columns, GATE_KINDS * LANES)
        return [slice(at, at + width) for at in range(0, self.columns, width)]

    def add(self, groups, away, total=None, first=None):
        chunks = len(groups[0])
        rows = sum(block.shape[0] for block in groups[0])
        extra = [] if total is None else [total]
        if first is not None:
            onehot, step, embed = first
            extra = [onehot, embed]

        def kernel(me_ref, weight_ref, *refs):
            extra_refs, refs, out_ref = refs[: len(extra)], refs[len(extra) : -1], refs[-1]
            blocks = [rows_of(refs[i * chunks : (i + 1) * chunks]) for i in range(len(away))]
            for columns in self.tiles():
                value = self.terms(me_ref, weight_ref, blocks, away, columns)
                if total is not None:
                    value = extra_refs[0][:, columns] + value
                if first is not None:
                    value = dot32(extra_refs[0][step], extra_refs[1][:, columns]) + value
                out_ref[:, columns] = value

        return call(
            kernel,
            [self.me, self.weight, *extra, *[block for group in groups for block in group]],
            [jax.ShapeDtypeStruct((rows, self.columns), jnp.float32)],
            2 * rows * self.columns * self.part * len(away),
        )[0]


def call(kernel, operands, outs, flops):
    size = sum(math.prod(out.shape) * out.dtype.itemsize for out in outs)
    return pl.pallas_call(
        kernel,
        in_specs=[pl.BlockSpec(memory_space=pltpu.SMEM)]
        + [pl.BlockSpec(memory_space=pltpu.VMEM)] * (len(operands) - 1),
        out_specs=[pl.BlockSpec(memory_space=pltpu.VMEM)] * len(outs),
        out_shape=outs,
        compiler_params=pltpu.CompilerParams(vmem_limit_bytes=SCRATCH),
        cost_estimate=pl.CostEstimate(flops=0, bytes_accessed=size, transcendentals=0),
    )(*operands)


def inter_of(gather, total, last, row, onehot, step, inter_embed, away):
    rows = last.shape[0]

    def kernel(me_ref, weight_ref, total_ref, last_ref, onehot_ref, embed_ref, out_ref):
        product = total_ref[row : row + rows] + gather.terms(
            me_ref, weight_ref, [last_ref[...]], [away], slice(None)
        )
        lookup = dot32(onehot_ref[step, row : row + rows], embed_ref[...])
        out_ref[...] = (lookup * product).astype(out_ref.dtype)

    return call(
        kernel,
        [gather.me, gather.weight, total, last, onehot, inter_embed],
        [jax.ShapeDtypeStruct((rows, gather.columns), jnp.bfloat16)],
        2 * rows * gather.columns * gather.part,
    )[0]


def state_of(gather, total, lasts, row, bias, cell, cell_row, mix, away):
    rows = sum(last.shape[0] for last in lasts)
    group = mix.shape[0]
    lanes = group // GATE_KINDS
    units = gather.columns // GATE_KINDS
    chunks = len(lasts)

    def kernel(me_ref, weight_ref, total_ref, bias_ref, cell_ref, mix_ref, *refs):
        last_refs, hidden_ref, cell_out_ref = refs[:chunks], refs[chunks], refs[chunks + 1]
        last = rows_of(last_refs)
        terms = []
        for columns in gather.tiles():
            full = total_ref[row : row + rows, columns] + gather.terms(
                me_ref, weight_ref, [last], [away], columns
            )
            full = full + bias_ref[:, columns]
            high = full.astype(jnp.bfloat16)
            terms += [high, (full - high.astype(jnp.float32)).astype(jnp.bfloat16)]
        mixed = dot32(jnp.concatenate(terms, 0), mix_ref[...])
        for g in range(len(terms) // 2):
            at = 2 * g * rows
            sums = mixed[at : at + rows] + mixed[at + rows : at + 2 * rows]
            here = slice(g * lanes, (g + 1) * lanes)
            hidden_ref[:, here], cell_out_ref[:, here] = update_state(
                [sums[:, j * lanes : (j + 1) * lanes] for j in range(GATE_KINDS)],
                cell_ref[cell_row : cell_row + rows, here],
            )

    return call(
        kernel,
        [gather.me, gather.weight, total, bias, cell, mix, *lasts],
        [
            jax.ShapeDtypeStruct((rows, units), jnp.bfloat16),
            jax.ShapeDtypeStruct((rows, units), jnp.float32),
        ],
        2 * rows * gather.columns * (gather.part + 2 * group),
    )


def after(block, total):
    return lax.optimization_barrier((block, total))[0]


def ringed(devices, chunks, first_chunks):
    ring = ring_of(devices)
    up = [(ring[i], ring[(i + 1) % devices]) for i in range(devices)]
    down = [(b, a) for a, b in up]
    away = [-((k + 1) // 2) if k % 2 else k // 2 for k in range(devices)]

    def local(
        byte_ids, h_start, c_start, inter_weight, inter_embed, gate_weight, gate_embed, gate_bias
    ):
        steps, streams = byte_ids.shape
        part = h_start.shape[1]
        me = jnp.full((1,), lax.axis_index("mp"), jnp.int32)
        to_inter = Gather(me, inter_weight, devices, part, True)
        to_gate = Gather(me, gate_weight, devices, part, False)
        mix = mix_matrix(GATE_KINDS * LANES)
        bias = gate_bias.reshape(1, -1)
        onehot = one_hot(byte_ids, inter_embed.shape[0])

        def gathered(blocks, gather, first=None):
            count = len(blocks)
            total = gather.add([blocks], away[:1], first=first)
            below = [lax.ppermute(block, "mp", up) for block in blocks]
            above = [lax.ppermute(block, "mp", down) for block in blocks]
            for k in range(1, devices - 1, 2):
                ready = total
                total = gather.add([below, above], away[k : k + 2], total)
                if k + 2 < devices - 1:
                    below = [lax.ppermute(after(block, ready), "mp", up) for block in below]
                    above = [lax.ppermute(after(block, ready), "mp", down) for block in above]
            if count == 1:
                half = blocks[0].shape[0] // 2
                lasts = [
                    lax.ppermute(after(below[0][:half], ready), "mp", up),
                    lax.ppermute(after(above[0][half:], ready), "mp", down),
                ]
            else:
                lasts = [
                    lax.ppermute(after(above[c], ready), "mp", down)
                    if c % 2
                    else lax.ppermute(after(below[c], ready), "mp", up)
                    for c in range(count)
                ]
            return total, lasts

        rows = streams // first_chunks
        hiddens = [h_start[c * rows : (c + 1) * rows] for c in range(first_chunks)]
        rows = streams // chunks
        cells = [(c_start, c * rows) for c in range(chunks)]
        for step in range(steps):
            total, lasts = gathered(hiddens, to_inter)
            inters = [
                inter_of(to_inter, total, last, c * rows, onehot, step, inter_embed, away[-1])
                for c, last in enumerate(lasts)
            ]
            total, lasts = gathered(inters, to_gate, (onehot, step, gate_embed))
            if step + 1 < steps:
                hiddens, updated = zip(
                    *[
                        state_of(to_gate, total, [last], c * rows, bias, *cells[c], mix, away[-1])
                        for c, last in enumerate(lasts)
                    ]
                )
                cells = [(cell, 0) for cell in updated]
            else:
                cell = cells[0][0]
                if cell.shape[0] < streams:
                    cell = jnp.concatenate([cell for cell, _ in cells], 0)
                return state_of(to_gate, total, lasts, 0, bias, cell, 0, mix, away[-1])

    return local


def solution(mesh):
    in_specs = (
        P(None, ("groups", "batch")),
        P(("groups", "batch"), "mp"),
        P(("groups", "batch"), "mp"),
        P("mp", None),
        P(None, "mp"),
        P(None, "mp"),
        P(None, "mp"),
        P("mp"),
    )
    out_specs = (P(("groups", "batch"), "mp"), P(("groups", "batch"), "mp"))
    devices = mesh.shape["mp"]
    local = ringed(devices, 2, 2) if 2 < devices <= MAX_RING else plain
    return jax.shard_map(local, mesh=mesh, in_specs=in_specs, out_specs=out_specs, check_vma=False)
```

```python
import jax
import jax.numpy as jnp
from jax import lax
from jax.experimental import pallas as pl
from jax.experimental.pallas import tpu as pltpu
from jax.sharding import PartitionSpec as P

GATE_KINDS = 4
LANES = 128
MAX_RING = 8
SCRATCH = 16 * 2**20


def plain(
    byte_ids, h_start, c_start, inter_weight, inter_embed, gate_weight, gate_embed, gate_bias
):
    hidden = h_start
    cell = c_start
    for step in range(byte_ids.shape[0]):
        rows_here = hidden.shape[0]
        onehot = one_hot(byte_ids[step], inter_embed.shape[0])
        product = lax.dot_general(
            lax.all_gather(hidden, "mp", axis=1, tiled=True),
            inter_weight,
            (((1,), (1,)), ((), ())),
            preferred_element_type=jnp.float32,
        )
        lookup = jnp.dot(onehot, inter_embed, preferred_element_type=jnp.float32)
        inter_vals = (lookup * product).astype(jnp.bfloat16)
        gate_sums = jnp.dot(
            lax.all_gather(inter_vals, "mp", axis=1, tiled=True),
            gate_weight,
            preferred_element_type=jnp.float32,
        )
        gate_sums = (
            gate_sums
            + jnp.dot(onehot, gate_embed, preferred_element_type=jnp.float32)
            + gate_bias[None, :]
        )
        gate_sums = gate_sums.reshape(rows_here, gate_sums.shape[1] // GATE_KINDS, GATE_KINDS)
        hidden, cell = update_state([gate_sums[:, :, j] for j in range(GATE_KINDS)], cell)
    return hidden, cell


def one_hot(ids, vocab):
    return (ids[..., None] == jnp.arange(vocab, dtype=jnp.int32)).astype(jnp.bfloat16)


def update_state(sums, cell):
    in_gate = jax.nn.sigmoid(sums[0])
    forget = jax.nn.sigmoid(sums[1])
    out_gate = jax.nn.sigmoid(sums[2])
    update = jnp.tanh(sums[3])
    cell = forget * cell + in_gate * update
    return (out_gate * jnp.tanh(cell)).astype(jnp.bfloat16), cell


def ring_of(devices):
    return list(range(0, devices, 2)) + list(range(devices - 1, 0, -2))


def ring_index(me, steps, devices):
    place = jnp.where(me % 2 == 0, me // 2, devices - 1 - me // 2)
    place = (place + steps + devices) % devices
    half = devices // 2
    return jnp.where(place < half, 2 * place, 2 * (devices - 1 - place) + 1)


def mix_matrix(group):
    lanes = group // GATE_KINDS
    source = jnp.arange(group, dtype=jnp.int32)[:, None]
    target = jnp.arange(group, dtype=jnp.int32)[None, :]
    wanted = (target % lanes) * GATE_KINDS + target // lanes
    return (source == wanted).astype(jnp.bfloat16)


def dot32(a, b):
    return jnp.dot(a, b, preferred_element_type=jnp.float32)


def dot32_turned(a, b):
    return lax.dot_general(a, b, (((1,), (1,)), ((), ())), preferred_element_type=jnp.float32)


def rows_of(refs):
    blocks = [ref[...] for ref in refs]
    return blocks[0] if len(blocks) == 1 else jnp.concatenate(blocks, 0)


class Gather:
    def __init__(self, me, weight, devices, part, turned):
        self.me, self.weight = me, weight
        self.devices, self.part, self.turned = devices, part, turned
        self.columns = weight.shape[0] if turned else weight.shape[1]

    def terms(self, me_ref, weight_ref, blocks, away, columns):
        total = None
        for block, steps in zip(blocks, away):
            start = pl.multiple_of(
                ring_index(me_ref[0], steps, self.devices) * self.part, self.part
            )
            if self.turned:
                term = dot32_turned(block, weight_ref[columns, pl.ds(start, self.part)])
            else:
                term = dot32(block, weight_ref[pl.ds(start, self.part), columns])
            total = term if total is None else total + term
        return total

    def tiles(self):
        width = min(self.columns, GATE_KINDS * LANES)
        return [slice(at, at + width) for at in range(0, self.columns, width)]

    def add(self, groups, away, total=None, first=None):
        chunks = len(groups[0])
        rows = sum(block.shape[0] for block in groups[0])
        extra = [] if total is None else [total]
        if first is not None:
            onehot, step, embed = first
            extra = [onehot, embed]

        def kernel(me_ref, weight_ref, *refs):
            extra_refs, refs, out_ref = refs[: len(extra)], refs[len(extra) : -1], refs[-1]
            blocks = [rows_of(refs[i * chunks : (i + 1) * chunks]) for i in range(len(away))]
            for columns in self.tiles():
                value = self.terms(me_ref, weight_ref, blocks, away, columns)
                if total is not None:
                    value = extra_refs[0][:, columns] + value
                if first is not None:
                    value = dot32(extra_refs[0][step], extra_refs[1][:, columns]) + value
                out_ref[:, columns] = value

        return call(
            kernel,
            [self.me, self.weight, *extra, *[block for group in groups for block in group]],
            [jax.ShapeDtypeStruct((rows, self.columns), jnp.float32)],
        )[0]


def call(kernel, operands, outs, space=pltpu.VMEM, scratch=()):
    return pl.pallas_call(
        kernel,
        in_specs=[pl.BlockSpec(memory_space=pltpu.SMEM)]
        + [pl.BlockSpec(memory_space=pltpu.VMEM)] * (len(operands) - 1),
        out_specs=[pl.BlockSpec(memory_space=space)] * len(outs),
        out_shape=outs,
        scratch_shapes=list(scratch),
        compiler_params=pltpu.CompilerParams(vmem_limit_bytes=SCRATCH),
    )(*operands)


def inter_of(gather, total, last, row, onehot, step, inter_embed, away):
    rows = last.shape[0]

    def kernel(me_ref, weight_ref, total_ref, onehot_ref, embed_ref, last_ref, out_ref):
        product = total_ref[row : row + rows] + gather.terms(
            me_ref, weight_ref, [last_ref[...]], [away], slice(None)
        )
        lookup = dot32(onehot_ref[step, row : row + rows], embed_ref[...])
        out_ref[...] = (lookup * product).astype(out_ref.dtype)

    return call(
        kernel,
        [gather.me, gather.weight, total, onehot, inter_embed, last],
        [jax.ShapeDtypeStruct((rows, gather.columns), jnp.bfloat16)],
    )[0]


def state_of(gather, total, last, row, bias, cell, cell_row, mix, away, done=None):
    rows = last.shape[0]
    group = mix.shape[0]
    lanes = group // GATE_KINDS
    units = gather.columns // GATE_KINDS
    ends = done is not None
    before = [array for pair in done for array in pair] if ends else []

    def kernel(me_ref, weight_ref, total_ref, bias_ref, cell_ref, mix_ref, last_ref, *refs):
        before_refs, refs = refs[: len(before)], refs[len(before) :]
        hidden_ref, cell_new_ref = refs[2:4] if ends else refs
        copies = []

        def send(sources, at):
            for source, target in zip(sources, refs):
                copy = pltpu.make_async_copy(
                    source, target.at[pl.ds(at, rows)], refs[4].at[len(copies)]
                )
                copy.start()
                copies.append(copy)

        for c in range(len(before) // 2):
            send(before_refs[2 * c : 2 * c + 2], c * rows)
        terms = []
        for columns in gather.tiles():
            full = total_ref[row : row + rows, columns] + gather.terms(
                me_ref, weight_ref, [last_ref[...]], [away], columns
            )
            full = full + bias_ref[:, columns]
            high = full.astype(jnp.bfloat16)
            terms += [high, (full - high.astype(jnp.float32)).astype(jnp.bfloat16)]
        mixed = dot32(jnp.concatenate(terms, 0), mix_ref[...])
        for g in range(len(terms) // 2):
            at = 2 * g * rows
            sums = mixed[at : at + rows] + mixed[at + rows : at + 2 * rows]
            here = slice(g * lanes, (g + 1) * lanes)
            hidden_ref[:, here], cell_new_ref[:, here] = update_state(
                [sums[:, j * lanes : (j + 1) * lanes] for j in range(GATE_KINDS)],
                cell_ref[cell_row : cell_row + rows, here],
            )
        if ends:
            send((hidden_ref, cell_new_ref), row)
        for copy in copies:
            copy.wait()

    operands = [gather.me, gather.weight, total, bias, cell, mix, last, *before]
    kinds = (jnp.bfloat16, jnp.float32)
    high = total.shape[0] if ends else rows
    shapes = [jax.ShapeDtypeStruct((high, units), kind) for kind in kinds]
    if not ends:
        return call(kernel, operands, shapes)
    return call(
        kernel,
        operands,
        shapes,
        pl.ANY,
        [pltpu.VMEM((rows, units), kind) for kind in kinds]
        + [pltpu.SemaphoreType.DMA((len(before) + 2,))],
    )


def after(block, total):
    return lax.optimization_barrier((block, total))[0]


def ringed(devices, chunks):
    ring = ring_of(devices)
    up = [(ring[i], ring[(i + 1) % devices]) for i in range(devices)]
    down = [(b, a) for a, b in up]
    away = [-((k + 1) // 2) if k % 2 else k // 2 for k in range(devices)]

    def local(
        byte_ids, h_start, c_start, inter_weight, inter_embed, gate_weight, gate_embed, gate_bias
    ):
        steps, streams = byte_ids.shape
        part = h_start.shape[1]
        if part % LANES or streams % (16 * chunks):
            return plain(
                byte_ids,
                h_start,
                c_start,
                inter_weight,
                inter_embed,
                gate_weight,
                gate_embed,
                gate_bias,
            )
        me = jnp.full((1,), lax.axis_index("mp"), jnp.int32)
        to_inter = Gather(me, inter_weight, devices, part, True)
        to_gate = Gather(me, gate_weight, devices, part, False)
        mix = mix_matrix(GATE_KINDS * LANES)
        bias = gate_bias.reshape(1, -1)
        onehot = one_hot(byte_ids, inter_embed.shape[0])

        def cut(array):
            rows = streams // chunks
            return [array[c * rows : (c + 1) * rows] for c in range(chunks)]

        def gathered(blocks, gather, first=None):
            total = gather.add([blocks], away[:1], first=first)
            below = [lax.ppermute(block, "mp", up) for block in blocks]
            above = [lax.ppermute(block, "mp", down) for block in blocks]
            if len(blocks) == 1:
                below, above = cut(below[0]), cut(above[0])
            for k in range(1, devices - 1, 2):
                ready = total
                total = gather.add([below, above], away[k : k + 2], total)
                if k + 2 < devices - 1:
                    below = [lax.ppermute(after(block, ready), "mp", up) for block in below]
                    above = [lax.ppermute(after(block, ready), "mp", down) for block in above]
            lasts = [
                lax.ppermute(above[c], "mp", down)
                if c % 2
                else lax.ppermute(below[c], "mp", up)
                for c in range(chunks)
            ]
            return total, lasts

        rows = streams // chunks
        hiddens = [h_start]
        cells = [(c_start, c * rows) for c in range(chunks)]
        for step in range(steps):
            total, lasts = gathered(hiddens, to_inter)
            inters = [
                inter_of(to_inter, total, last, c * rows, onehot, step, inter_embed, away[-1])
                for c, last in enumerate(lasts)
            ]
            total, lasts = gathered(inters, to_gate, (onehot, step, gate_embed))
            updates = []
            for c, last in enumerate(lasts):
                done = updates if step + 1 == steps and c + 1 == chunks else None
                updates.append(
                    state_of(to_gate, total, last, c * rows, bias, *cells[c], mix, away[-1], done)
                )
            hiddens = [hidden for hidden, _ in updates]
            cells = [(cell, 0) for _, cell in updates]
        return tuple(updates[-1])

    return local


def solution(mesh):
    in_specs = (
        P(None, ("groups", "batch")),
        P(("groups", "batch"), "mp"),
        P(("groups", "batch"), "mp"),
        P("mp", None),
        P(None, "mp"),
        P(None, "mp"),
        P(None, "mp"),
        P("mp"),
    )
    out_specs = (P(("groups", "batch"), "mp"), P(("groups", "batch"), "mp"))
    devices = mesh.shape["mp"]
    local = ringed(devices, 2) if 2 < devices <= MAX_RING else plain
    return jax.shard_map(local, mesh=mesh, in_specs=in_specs, out_specs=out_specs, check_vma=False)
```

```python
import jax
import jax.numpy as jnp
from jax import lax
from jax.experimental import pallas as pl
from jax.experimental.pallas import tpu as pltpu
from jax.sharding import PartitionSpec as P

GATE_KINDS = 4
LANES = 128
MAX_RING = 8
SCRATCH = 12 * 2**20


def plain(
    byte_ids, h_start, c_start, inter_weight, inter_embed, gate_weight, gate_embed, gate_bias
):
    hidden = h_start
    cell = c_start
    for step in range(byte_ids.shape[0]):
        rows_here = hidden.shape[0]
        onehot = one_hot(byte_ids[step], inter_embed.shape[0])
        product = lax.dot_general(
            lax.all_gather(hidden, "mp", axis=1, tiled=True),
            inter_weight,
            (((1,), (1,)), ((), ())),
            preferred_element_type=jnp.float32,
        )
        lookup = jnp.dot(onehot, inter_embed, preferred_element_type=jnp.float32)
        inter_vals = (lookup * product).astype(jnp.bfloat16)
        gate_sums = jnp.dot(
            lax.all_gather(inter_vals, "mp", axis=1, tiled=True),
            gate_weight,
            preferred_element_type=jnp.float32,
        )
        gate_sums = (
            gate_sums
            + jnp.dot(onehot, gate_embed, preferred_element_type=jnp.float32)
            + gate_bias[None, :]
        )
        gate_sums = gate_sums.reshape(rows_here, gate_sums.shape[1] // GATE_KINDS, GATE_KINDS)
        hidden, cell = update_state([gate_sums[:, :, j] for j in range(GATE_KINDS)], cell)
    return hidden, cell


def one_hot(ids, vocab):
    return (ids[..., None] == jnp.arange(vocab, dtype=jnp.int32)).astype(jnp.bfloat16)


def update_state(sums, cell):
    in_gate = jax.nn.sigmoid(sums[0])
    forget = jax.nn.sigmoid(sums[1])
    out_gate = jax.nn.sigmoid(sums[2])
    update = jnp.tanh(sums[3])
    cell = forget * cell + in_gate * update
    return (out_gate * jnp.tanh(cell)).astype(jnp.bfloat16), cell


def ring_of(devices):
    return list(range(0, devices, 2)) + list(range(devices - 1, 0, -2))


def ring_index(me, steps, devices):
    place = jnp.where(me % 2 == 0, me // 2, devices - 1 - me // 2)
    place = (place + steps + devices) % devices
    half = devices // 2
    return jnp.where(place < half, 2 * place, 2 * (devices - 1 - place) + 1)


def mix_matrix(group):
    lanes = group // GATE_KINDS
    source = jnp.arange(group, dtype=jnp.int32)[:, None]
    target = jnp.arange(group, dtype=jnp.int32)[None, :]
    wanted = (target % lanes) * GATE_KINDS + target // lanes
    return (source == wanted).astype(jnp.bfloat16)


def dot32(a, b):
    return jnp.dot(a, b, preferred_element_type=jnp.float32)


def dot32_turned(a, b):
    return lax.dot_general(a, b, (((1,), (1,)), ((), ())), preferred_element_type=jnp.float32)


def rows_of(refs):
    blocks = [ref[...] for ref in refs]
    return blocks[0] if len(blocks) == 1 else jnp.concatenate(blocks, 0)


class Gather:
    def __init__(self, me, weight, devices, part, turned):
        self.me, self.weight = me, weight
        self.devices, self.part, self.turned = devices, part, turned
        self.columns = weight.shape[0] if turned else weight.shape[1]

    def terms(self, me_ref, weight_ref, blocks, away, columns):
        total = None
        for block, steps in zip(blocks, away):
            start = pl.multiple_of(
                ring_index(me_ref[0], steps, self.devices) * self.part, self.part
            )
            if self.turned:
                term = dot32_turned(block, weight_ref[columns, pl.ds(start, self.part)])
            else:
                term = dot32(block, weight_ref[pl.ds(start, self.part), columns])
            total = term if total is None else total + term
        return total

    def tiles(self):
        width = min(self.columns, (2 if self.turned else GATE_KINDS) * LANES)
        return [slice(at, at + width) for at in range(0, self.columns, width)]

    def add(self, groups, away, total=None, first=None):
        chunks = len(groups[0])
        rows = sum(block.shape[0] for block in groups[0])
        extra = [] if total is None else [total]
        if first is not None:
            onehot, step, embed = first
            extra = [onehot, embed]

        def kernel(me_ref, weight_ref, *refs):
            extra_refs, refs, out_ref = refs[: len(extra)], refs[len(extra) : -1], refs[-1]
            blocks = [rows_of(refs[i * chunks : (i + 1) * chunks]) for i in range(len(away))]
            for columns in self.tiles():
                value = self.terms(me_ref, weight_ref, blocks, away, columns)
                if total is not None:
                    value = extra_refs[0][:, columns] + value
                if first is not None:
                    value = dot32(extra_refs[0][step], extra_refs[1][:, columns]) + value
                out_ref[:, columns] = value

        return call(
            kernel,
            [self.me, self.weight, *extra, *[block for group in groups for block in group]],
            [jax.ShapeDtypeStruct((rows, self.columns), jnp.float32)],
        )[0]


def call(kernel, operands, outs, space=pltpu.VMEM, scratch=()):
    return pl.pallas_call(
        kernel,
        in_specs=[pl.BlockSpec(memory_space=pltpu.SMEM)]
        + [pl.BlockSpec(memory_space=pltpu.VMEM)] * (len(operands) - 1),
        out_specs=[pl.BlockSpec(memory_space=space)] * len(outs),
        out_shape=outs,
        scratch_shapes=list(scratch),
        compiler_params=pltpu.CompilerParams(vmem_limit_bytes=SCRATCH),
    )(*operands)


def inter_of(gather, total, last, row, onehot, step, inter_embed, away):
    rows = last.shape[0]

    def kernel(me_ref, weight_ref, total_ref, onehot_ref, embed_ref, last_ref, out_ref):
        product = total_ref[row : row + rows] + gather.terms(
            me_ref, weight_ref, [last_ref[...]], [away], slice(None)
        )
        lookup = dot32(onehot_ref[step, row : row + rows], embed_ref[...])
        out_ref[...] = (lookup * product).astype(out_ref.dtype)

    return call(
        kernel,
        [gather.me, gather.weight, total, onehot, inter_embed, last],
        [jax.ShapeDtypeStruct((rows, gather.columns), jnp.bfloat16)],
    )[0]


def state_of(gather, total, last, row, bias, cell, cell_row, mix, away, done=None):
    rows = last.shape[0]
    group = mix.shape[0]
    lanes = group // GATE_KINDS
    units = gather.columns // GATE_KINDS
    ends = done is not None
    before = [array for pair in done for array in pair] if ends else []

    def kernel(me_ref, weight_ref, total_ref, bias_ref, cell_ref, mix_ref, last_ref, *refs):
        before_refs, refs = refs[: len(before)], refs[len(before) :]
        hidden_ref, cell_new_ref = refs[2:4] if ends else refs
        copies = []

        def send(sources, at):
            for source, target in zip(sources, refs):
                copy = pltpu.make_async_copy(
                    source, target.at[pl.ds(at, rows)], refs[4].at[len(copies)]
                )
                copy.start()
                copies.append(copy)

        for c in range(len(before) // 2):
            send(before_refs[2 * c : 2 * c + 2], c * rows)
        terms = []
        for columns in gather.tiles():
            full = total_ref[row : row + rows, columns] + gather.terms(
                me_ref, weight_ref, [last_ref[...]], [away], columns
            )
            full = full + bias_ref[:, columns]
            high = full.astype(jnp.bfloat16)
            terms += [high, (full - high.astype(jnp.float32)).astype(jnp.bfloat16)]
        mixed = dot32(jnp.concatenate(terms, 0), mix_ref[...])
        for g in range(len(terms) // 2):
            at = 2 * g * rows
            sums = mixed[at : at + rows] + mixed[at + rows : at + 2 * rows]
            here = slice(g * lanes, (g + 1) * lanes)
            hidden_ref[:, here], cell_new_ref[:, here] = update_state(
                [sums[:, j * lanes : (j + 1) * lanes] for j in range(GATE_KINDS)],
                cell_ref[cell_row : cell_row + rows, here],
            )
        if ends:
            send((hidden_ref, cell_new_ref), row)
        for copy in copies:
            copy.wait()

    operands = [gather.me, gather.weight, total, bias, cell, mix, last, *before]
    kinds = (jnp.bfloat16, jnp.float32)
    high = total.shape[0] if ends else rows
    shapes = [jax.ShapeDtypeStruct((high, units), kind) for kind in kinds]
    if not ends:
        return call(kernel, operands, shapes)
    return call(
        kernel,
        operands,
        shapes,
        pl.ANY,
        [pltpu.VMEM((rows, units), kind) for kind in kinds]
        + [pltpu.SemaphoreType.DMA((len(before) + 2,))],
    )


def after(block, total):
    return lax.optimization_barrier((block, total))[0]


def ringed(devices, chunks):
    ring = ring_of(devices)
    up = [(ring[i], ring[(i + 1) % devices]) for i in range(devices)]
    down = [(b, a) for a, b in up]
    away = [-((k + 1) // 2) if k % 2 else k // 2 for k in range(devices)]

    def local(
        byte_ids, h_start, c_start, inter_weight, inter_embed, gate_weight, gate_embed, gate_bias
    ):
        steps, streams = byte_ids.shape
        part = h_start.shape[1]
        if part % LANES or streams % (16 * chunks):
            return plain(
                byte_ids,
                h_start,
                c_start,
                inter_weight,
                inter_embed,
                gate_weight,
                gate_embed,
                gate_bias,
            )
        me = jnp.full((1,), lax.axis_index("mp"), jnp.int32)
        to_inter = Gather(me, inter_weight, devices, part, True)
        to_gate = Gather(me, gate_weight, devices, part, False)
        mix = mix_matrix(GATE_KINDS * LANES)
        bias = gate_bias.reshape(1, -1)
        onehot = one_hot(byte_ids, inter_embed.shape[0])

        def cut(array):
            rows = streams // chunks
            return [array[c * rows : (c + 1) * rows] for c in range(chunks)]

        def gathered(blocks, gather, first=None):
            total = gather.add([blocks], away[:1], first=first)
            below = [lax.ppermute(block, "mp", up) for block in blocks]
            above = [lax.ppermute(block, "mp", down) for block in blocks]
            if len(blocks) == 1:
                below, above = cut(below[0]), cut(above[0])
            for k in range(1, devices - 1, 2):
                ready = total
                total = gather.add([below, above], away[k : k + 2], total)
                if k + 2 < devices - 1:
                    above = [lax.ppermute(after(block, ready), "mp", down) for block in above]
                    below = [lax.ppermute(after(block, ready), "mp", up) for block in below]
            lasts = [
                lax.ppermute(above[c], "mp", down)
                if c % 2
                else lax.ppermute(below[c], "mp", up)
                for c in range(chunks)
            ]
            return total, lasts

        rows = streams // chunks
        hiddens = [h_start]
        cells = [(c_start, c * rows) for c in range(chunks)]
        for step in range(steps):
            total, lasts = gathered(hiddens, to_inter)
            inters = [
                inter_of(to_inter, total, last, c * rows, onehot, step, inter_embed, away[-1])
                for c, last in enumerate(lasts)
            ]
            total, lasts = gathered(inters, to_gate, (onehot, step, gate_embed))
            updates = []
            for c, last in enumerate(lasts):
                done = updates if step + 1 == steps and c + 1 == chunks else None
                updates.append(
                    state_of(to_gate, total, last, c * rows, bias, *cells[c], mix, away[-1], done)
                )
            hiddens = [hidden for hidden, _ in updates]
            cells = [(cell, 0) for _, cell in updates]
        return tuple(updates[-1])

    return local


def solution(mesh):
    in_specs = (
        P(None, ("groups", "batch")),
        P(("groups", "batch"), "mp"),
        P(("groups", "batch"), "mp"),
        P("mp", None),
        P(None, "mp"),
        P(None, "mp"),
        P(None, "mp"),
        P("mp"),
    )
    out_specs = (P(("groups", "batch"), "mp"), P(("groups", "batch"), "mp"))
    devices = mesh.shape["mp"]
    local = ringed(devices, 2) if 2 < devices <= MAX_RING else plain
    return jax.shard_map(local, mesh=mesh, in_specs=in_specs, out_specs=out_specs, check_vma=False)
```

```python
import jax
import jax.numpy as jnp
from jax import lax
from jax.experimental import pallas as pl
from jax.experimental.pallas import tpu as pltpu
from jax.sharding import PartitionSpec as P

GATE_KINDS = 4
LANES = 128
MAX_RING = 8
SCRATCH = 16 * 2**20


def plain(
    byte_ids, h_start, c_start, inter_weight, inter_embed, gate_weight, gate_embed, gate_bias
):
    hidden = h_start
    cell = c_start
    for step in range(byte_ids.shape[0]):
        rows_here = hidden.shape[0]
        onehot = one_hot(byte_ids[step], inter_embed.shape[0])
        product = lax.dot_general(
            lax.all_gather(hidden, "mp", axis=1, tiled=True),
            inter_weight,
            (((1,), (1,)), ((), ())),
            preferred_element_type=jnp.float32,
        )
        lookup = jnp.dot(onehot, inter_embed, preferred_element_type=jnp.float32)
        inter_vals = (lookup * product).astype(jnp.bfloat16)
        gate_sums = jnp.dot(
            lax.all_gather(inter_vals, "mp", axis=1, tiled=True),
            gate_weight,
            preferred_element_type=jnp.float32,
        )
        gate_sums = (
            gate_sums
            + jnp.dot(onehot, gate_embed, preferred_element_type=jnp.float32)
            + gate_bias[None, :]
        )
        gate_sums = gate_sums.reshape(rows_here, gate_sums.shape[1] // GATE_KINDS, GATE_KINDS)
        hidden, cell = update_state([gate_sums[:, :, j] for j in range(GATE_KINDS)], cell)
    return hidden, cell


def one_hot(ids, vocab):
    return (ids[..., None] == jnp.arange(vocab, dtype=jnp.int32)).astype(jnp.bfloat16)


def update_state(sums, cell):
    in_gate = jax.nn.sigmoid(sums[0])
    forget = jax.nn.sigmoid(sums[1])
    out_gate = jax.nn.sigmoid(sums[2])
    update = jnp.tanh(sums[3])
    cell = forget * cell + in_gate * update
    return (out_gate * jnp.tanh(cell)).astype(jnp.bfloat16), cell


def ring_of(devices):
    return list(range(0, devices, 2)) + list(range(devices - 1, 0, -2))


def ring_index(me, steps, devices):
    place = jnp.where(me % 2 == 0, me // 2, devices - 1 - me // 2)
    place = (place + steps + devices) % devices
    half = devices // 2
    return jnp.where(place < half, 2 * place, 2 * (devices - 1 - place) + 1)


def mix_matrix(group):
    lanes = group // GATE_KINDS
    source = jnp.arange(group, dtype=jnp.int32)[:, None]
    target = jnp.arange(group, dtype=jnp.int32)[None, :]
    wanted = (target % lanes) * GATE_KINDS + target // lanes
    return (source == wanted).astype(jnp.bfloat16)


def dot32(a, b):
    return jnp.dot(a, b, preferred_element_type=jnp.float32)


def dot32_turned(a, b):
    return lax.dot_general(a, b, (((1,), (1,)), ((), ())), preferred_element_type=jnp.float32)


def rows_of(refs):
    blocks = [ref[...] for ref in refs]
    return blocks[0] if len(blocks) == 1 else jnp.concatenate(blocks, 0)


class Gather:
    def __init__(self, me, weight, devices, part, turned):
        self.me, self.weight = me, weight
        self.devices, self.part, self.turned = devices, part, turned
        self.columns = weight.shape[0] if turned else weight.shape[1]

    def terms(self, me_ref, weight_ref, blocks, away, columns):
        total = None
        for block, steps in zip(blocks, away):
            start = pl.multiple_of(
                ring_index(me_ref[0], steps, self.devices) * self.part, self.part
            )
            if self.turned:
                term = dot32_turned(block, weight_ref[columns, pl.ds(start, self.part)])
            else:
                term = dot32(block, weight_ref[pl.ds(start, self.part), columns])
            total = term if total is None else total + term
        return total

    def tiles(self, width=GATE_KINDS * LANES):
        width = min(self.columns, width)
        return [slice(at, at + width) for at in range(0, self.columns, width)]

    def add(self, groups, away, total=None, first=None):
        chunks = len(groups[0])
        rows = sum(block.shape[0] for block in groups[0])
        extra = [] if total is None else [total]
        if first is not None:
            onehot, step, embed = first
            extra = [onehot, embed]

        def kernel(me_ref, weight_ref, *refs):
            extra_refs, refs, out_ref = refs[: len(extra)], refs[len(extra) : -1], refs[-1]
            blocks = [rows_of(refs[i * chunks : (i + 1) * chunks]) for i in range(len(away))]
            for columns in self.tiles(2 * LANES):
                value = self.terms(me_ref, weight_ref, blocks, away, columns)
                if total is not None:
                    value = extra_refs[0][:, columns] + value
                if first is not None:
                    value = dot32(extra_refs[0][step], extra_refs[1][:, columns]) + value
                out_ref[:, columns] = value

        return call(
            kernel,
            [self.me, self.weight, *extra, *[block for group in groups for block in group]],
            [jax.ShapeDtypeStruct((rows, self.columns), jnp.float32)],
        )[0]


def call(kernel, operands, outs, space=pltpu.VMEM, scratch=()):
    return pl.pallas_call(
        kernel,
        in_specs=[pl.BlockSpec(memory_space=pltpu.SMEM)]
        + [pl.BlockSpec(memory_space=pltpu.VMEM)] * (len(operands) - 1),
        out_specs=[pl.BlockSpec(memory_space=space)] * len(outs),
        out_shape=outs,
        scratch_shapes=list(scratch),
        compiler_params=pltpu.CompilerParams(vmem_limit_bytes=SCRATCH),
    )(*operands)


def inter_of(gather, total, last, row, onehot, step, inter_embed, away):
    rows = last.shape[0]

    def kernel(me_ref, weight_ref, total_ref, onehot_ref, embed_ref, last_ref, out_ref):
        product = total_ref[row : row + rows] + gather.terms(
            me_ref, weight_ref, [last_ref[...]], [away], slice(None)
        )
        lookup = dot32(onehot_ref[step, row : row + rows], embed_ref[...])
        out_ref[...] = (lookup * product).astype(out_ref.dtype)

    return call(
        kernel,
        [gather.me, gather.weight, total, onehot, inter_embed, last],
        [jax.ShapeDtypeStruct((rows, gather.columns), jnp.bfloat16)],
    )[0]


def state_of(gather, total, last, row, bias, cell, cell_row, mix, away, done=None):
    rows = last.shape[0]
    group = mix.shape[0]
    lanes = group // GATE_KINDS
    units = gather.columns // GATE_KINDS
    ends = done is not None
    before = [array for pair in done for array in pair] if ends else []

    def kernel(me_ref, weight_ref, total_ref, bias_ref, cell_ref, mix_ref, last_ref, *refs):
        before_refs, refs = refs[: len(before)], refs[len(before) :]
        hidden_ref, cell_new_ref = refs[2:4] if ends else refs
        copies = []

        def send(sources, at):
            for source, target in zip(sources, refs):
                copy = pltpu.make_async_copy(
                    source, target.at[pl.ds(at, rows)], refs[4].at[len(copies)]
                )
                copy.start()
                copies.append(copy)

        for c in range(len(before) // 2):
            send(before_refs[2 * c : 2 * c + 2], c * rows)
        terms = []
        for columns in gather.tiles():
            full = total_ref[row : row + rows, columns] + gather.terms(
                me_ref, weight_ref, [last_ref[...]], [away], columns
            )
            full = full + bias_ref[:, columns]
            high = full.astype(jnp.bfloat16)
            terms += [high, (full - high.astype(jnp.float32)).astype(jnp.bfloat16)]
        mixed = dot32(jnp.concatenate(terms, 0), mix_ref[...])
        for g in range(len(terms) // 2):
            at = 2 * g * rows
            sums = mixed[at : at + rows] + mixed[at + rows : at + 2 * rows]
            here = slice(g * lanes, (g + 1) * lanes)
            hidden_ref[:, here], cell_new_ref[:, here] = update_state(
                [sums[:, j * lanes : (j + 1) * lanes] for j in range(GATE_KINDS)],
                cell_ref[cell_row : cell_row + rows, here],
            )
        if ends:
            send((hidden_ref, cell_new_ref), row)
        for copy in copies:
            copy.wait()

    operands = [gather.me, gather.weight, total, bias, cell, mix, last, *before]
    kinds = (jnp.bfloat16, jnp.float32)
    high = total.shape[0] if ends else rows
    shapes = [jax.ShapeDtypeStruct((high, units), kind) for kind in kinds]
    if not ends:
        return call(kernel, operands, shapes)
    return call(
        kernel,
        operands,
        shapes,
        pl.ANY,
        [pltpu.VMEM((rows, units), kind) for kind in kinds]
        + [pltpu.SemaphoreType.DMA((len(before) + 2,))],
    )


def after(block, total):
    return lax.optimization_barrier((block, total))[0]


def ringed(devices, chunks):
    ring = ring_of(devices)
    up = [(ring[i], ring[(i + 1) % devices]) for i in range(devices)]
    down = [(b, a) for a, b in up]
    away = [-((k + 1) // 2) if k % 2 else k // 2 for k in range(devices)]

    def local(
        byte_ids, h_start, c_start, inter_weight, inter_embed, gate_weight, gate_embed, gate_bias
    ):
        steps, streams = byte_ids.shape
        part = h_start.shape[1]
        if part % LANES or streams % (16 * chunks):
            return plain(
                byte_ids,
                h_start,
                c_start,
                inter_weight,
                inter_embed,
                gate_weight,
                gate_embed,
                gate_bias,
            )
        me = jnp.full((1,), lax.axis_index("mp"), jnp.int32)
        to_inter = Gather(me, inter_weight, devices, part, True)
        to_gate = Gather(me, gate_weight, devices, part, False)
        mix = mix_matrix(GATE_KINDS * LANES)
        bias = gate_bias.reshape(1, -1)
        onehot = one_hot(byte_ids, inter_embed.shape[0])

        def cut(array):
            rows = streams // chunks
            return [array[c * rows : (c + 1) * rows] for c in range(chunks)]

        def gathered(blocks, gather, first=None):
            total = gather.add([blocks], away[:1], first=first)
            below = [lax.ppermute(block, "mp", up) for block in blocks]
            above = [lax.ppermute(block, "mp", down) for block in blocks]
            if len(blocks) == 1:
                below, above = cut(below[0]), cut(above[0])
            for k in range(1, devices - 1, 2):
                ready = total
                total = gather.add([below, above], away[k : k + 2], total)
                if k + 2 < devices - 1:
                    below = [lax.ppermute(after(block, ready), "mp", up) for block in below]
                    above = [lax.ppermute(after(block, ready), "mp", down) for block in above]
            lasts = [
                lax.ppermute(above[c], "mp", down)
                if c % 2
                else lax.ppermute(below[c], "mp", up)
                for c in range(chunks)
            ]
            return total, lasts

        rows = streams // chunks
        hiddens = [h_start]
        cells = [(c_start, c * rows) for c in range(chunks)]
        for step in range(steps):
            total, lasts = gathered(hiddens, to_inter)
            inters = [
                inter_of(to_inter, total, last, c * rows, onehot, step, inter_embed, away[-1])
                for c, last in enumerate(lasts)
            ]
            total, lasts = gathered(inters, to_gate, (onehot, step, gate_embed))
            updates = []
            for c, last in enumerate(lasts):
                done = updates if step + 1 == steps and c + 1 == chunks else None
                updates.append(
                    state_of(to_gate, total, last, c * rows, bias, *cells[c], mix, away[-1], done)
                )
            hiddens = [hidden for hidden, _ in updates]
            cells = [(cell, 0) for _, cell in updates]
        return tuple(updates[-1])

    return local


def solution(mesh):
    in_specs = (
        P(None, ("groups", "batch")),
        P(("groups", "batch"), "mp"),
        P(("groups", "batch"), "mp"),
        P("mp", None),
        P(None, "mp"),
        P(None, "mp"),
        P(None, "mp"),
        P("mp"),
    )
    out_specs = (P(("groups", "batch"), "mp"), P(("groups", "batch"), "mp"))
    devices = mesh.shape["mp"]
    local = ringed(devices, 2) if 2 < devices <= MAX_RING else plain
    return jax.shard_map(local, mesh=mesh, in_specs=in_specs, out_specs=out_specs, check_vma=False)
```
